256 devices in a mesh: grp: 8 (over x, y_hi), tp: 8 (over z), dp: 4 (over y_lo, core).
Axes of the slice: x: 4, y: 4 (y_hi: 2, y_lo: 2; y = y_hi * 2 + y_lo), z: 8, core: 2. Of those that a mesh axis runs over, the one named last changes fastest.
Arguments:
- prompt_hidden: bfloat16 [8192, 5120], P(('dp', 'grp'), 'tp'), parts along dimension 0, may hold values from -6 to 6
- w_kv: bfloat16 [5120, 2048], P('tp'), may hold values from -0.078125 to 0.078125
- resp_q: bfloat16 [32, 256, 8192], P(('dp', 'grp'), None, 'tp'), parts along dimension 0, may hold values from -28 to 28
- resp_kv: bfloat16 [32, 256, 2048], P(('dp', 'grp'), None, 'tp'), parts along dimension 0, may hold values from -28 to 28
- d_out: bfloat16 [32, 256, 8192], P(('dp', 'grp'), None, 'tp'), parts along dimension 0, may hold values from -96 to 96
- lengths: int32 [32], P(('dp', 'grp')), parts along dimension 0, may hold values from 32 to 256, as said below
Outputs:
- d_q: bfloat16 [32, 256, 8192], P(('dp', 'grp'), None, 'tp'), parts along dimension 0
- d_kv_resp: bfloat16 [32, 256, 2048], P(('dp', 'grp'), None, 'tp'), parts along dimension 0
- d_hidden: bfloat16 [8192, 5120], P(('dp', 'grp'), 'tp'), parts along dimension 0
- d_wkv: float32 [20480, 2048], P(('dp', 'tp'), 'grp'), parts along dimension 0
The draws below stay inside these ranges and needn't reach their ends.
There are 4 independent parts, one for each index of `dp`. The reference program is written for one: setup_inputs(seed, part) draws one part's arguments, and reference() takes and returns one part's arrays. A program takes and returns all parts, laid end to end along the dimension named above; an argument that names none is the same for every part. Nothing has to cross between parts.
Inputs may be any that keep to these rules, and one draw needn't show every extreme that they name: `lengths`: the first response of every prompt has 256 live tokens.
All inputs are finite; a program needn't handle non-finite values.
Results may differ from the reference program's by a relative error of at most 0.035.
The reference program's roundings to bfloat16 on the way count: a program that leaves them out, or rounds other values in their place, can miss the bound.
Values may be sent and summed in bfloat16 or wider, within the bound.
A program may use at most 128 MiB of HBM per device.

```python
import jax
import jax.numpy as jnp
from jax import lax

D = 5120
QH = 64
KVH = 8
HD = 128
GQ = 8
KVW = 2048
PROMPT = 2048
LEN = 256
RESP = 8


def draw_resp_q(key, part):
    key = jax.random.fold_in(key, 21)
    return jnp.clip(jax.random.normal(key, (RESP, LEN, QH * HD), jnp.float32), -6.0, 6.0).astype(jnp.bfloat16)


def draw_resp_kv(key, part):
    key = jax.random.fold_in(key, 33)
    return jnp.clip(jax.random.normal(key, (RESP, LEN, KVW), jnp.float32), -6.0, 6.0).astype(jnp.bfloat16)


def draw_lengths(key, part):
    key = jax.random.fold_in(key, 5)
    counts = jax.random.randint(key, (RESP,), LEN // 8, LEN + 1)
    return jnp.where(jnp.arange(RESP) == 0, LEN, counts).astype(jnp.int32)


def steps_of(rng, extent, pieces, smallest, top_value):
    loudness = 1.0
    for position, shards_of in pieces:
        heights = jax.random.uniform(jax.random.fold_in(jax.random.fold_in(rng, 6), position), (shards_of,), jnp.float32, smallest / len(pieces), top_value / len(pieces))
        loudness = loudness * jnp.repeat(jnp.exp(heights), extent[position] // shards_of).reshape((-1,) + (1,) * (len(extent) - 1 - position))
    return loudness


def normal_values(stream_key, dims, spread, bound, pieces=(), held_as=jnp.bfloat16):
    values = spread * jax.random.normal(stream_key, dims, jnp.float32)
    if pieces:
        values = values * steps_of(stream_key, dims, pieces, -0.22, 0.18)
    return jnp.clip(values, -bound, bound).astype(held_as)


def setup_inputs(seed: int = 0, part: int = 0) -> dict:
    streams_of = jax.random.split(jax.random.key(seed), 7)
    part_splits = jax.random.split(jax.random.fold_in(streams_of[6], part), 7)
    return {
        "prompt_hidden": normal_values(part_splits[0], (PROMPT, D), 1.0, 6.0, ((0, 8), (1, 8))),
        "w_kv": normal_values(streams_of[1], (D, KVW), D ** -0.5, 0.078125, ((0, 8),)),
        "resp_q": draw_resp_q(jax.random.fold_in(jax.random.fold_in(streams_of[6], part), 71), part),
        "resp_kv": draw_resp_kv(jax.random.fold_in(jax.random.fold_in(streams_of[6], part), 71), part),
        "d_out": normal_values(part_splits[4], (RESP, LEN, QH * HD), 16.0, 96.0, ((0, 8), (2, 8))),
        "lengths": draw_lengths(jax.random.fold_in(jax.random.fold_in(streams_of[6], part), 71), part),
    }


rope_theta = 1000000.0


def angles(positions):
    ladder = jnp.arange(HD // 2).astype(jnp.float32)
    frequency = rope_theta ** (-2.0 * ladder / HD)
    turned = positions.astype(jnp.float32)[:, None] * frequency[None, :]
    return jnp.cos(turned), jnp.sin(turned)


def rotate(values, cosine, sine_part):
    half_width = values.shape[-1] // 2
    first_half = values[..., :half_width]
    second = values[..., half_width:]
    return jnp.concatenate([first_half * cosine - second * sine_part, second * cosine + first_half * sine_part], -1)


def one_group(q_group, key_rows, value_rows, grad_group):
    score_scale = HD ** -0.5
    query_pos = jnp.arange(LEN)[:, None]
    key_pos = jnp.arange(PROMPT + LEN)[None, :]
    visible = (key_pos < PROMPT) | (key_pos - PROMPT <= query_pos)
    query_f = q_group.astype(jnp.float32).transpose(1, 0, 2)
    grad_f = grad_group.astype(jnp.float32).transpose(1, 0, 2)
    key_f = key_rows.astype(jnp.float32)
    value_f = value_rows.astype(jnp.float32)
    scores = jnp.einsum("gtd,cd->gtc", query_f, key_f) * score_scale
    scores = jnp.where(visible[None], scores, -jnp.inf)
    attend = jax.nn.softmax(scores, axis=-1)
    attend_b = lax.optimization_barrier(attend.astype(jnp.bfloat16)).astype(jnp.float32)
    output = lax.optimization_barrier(jnp.einsum("gtc,cd->gtd", attend_b, value_f).astype(jnp.bfloat16)).astype(jnp.float32)
    delta_row = jnp.sum(grad_f * output, -1)
    d_attend = jnp.einsum("gtd,cd->gtc", grad_f, value_f)
    d_score = lax.optimization_barrier((attend * (d_attend - delta_row[..., None])).astype(jnp.bfloat16)).astype(jnp.float32)
    d_query = jnp.einsum("gtc,cd->gtd", d_score, key_f) * score_scale
    d_key = jnp.einsum("gtc,gtd->cd", d_score, query_f) * score_scale
    d_value = jnp.einsum("gtc,gtd->cd", attend_b, grad_f)
    return d_query, d_key, d_value


def reference(prompt_hidden, w_kv, resp_q, resp_kv, d_out, lengths):
    projected = jnp.dot(prompt_hidden, w_kv, preferred_element_type=jnp.float32).reshape(PROMPT, KVH, 2, HD)
    cos_prompt, sin_prompt = angles(jnp.arange(PROMPT))
    prompt_keys = rotate(projected[:, :, 0], cos_prompt[:, None], sin_prompt[:, None])
    prefix = jnp.stack([prompt_keys, projected[:, :, 1]], 2).astype(jnp.bfloat16)
    cos_resp, sin_resp = angles(PROMPT + jnp.arange(LEN))
    queries = rotate(resp_q.reshape(RESP, LEN, QH, HD).astype(jnp.float32), cos_resp[None, :, None], sin_resp[None, :, None]).astype(jnp.bfloat16)
    own_pairs = resp_kv.reshape(RESP, LEN, KVH, 2, HD)
    own_keys = rotate(own_pairs[:, :, :, 0].astype(jnp.float32), cos_resp[None, :, None], sin_resp[None, :, None]).astype(jnp.bfloat16)
    own_values = own_pairs[:, :, :, 1]
    live_rows = jnp.arange(LEN)[None, :] < lengths[:, None]
    masked = jnp.where(live_rows[:, :, None], d_out, jnp.zeros_like(d_out)).reshape(RESP, LEN, QH, HD)

    def one_pair(flat_index):
        which_resp = (flat_index // KVH).astype(jnp.int32)
        which_head = (flat_index % KVH).astype(jnp.int32)
        head_start = (which_head * GQ).astype(jnp.int32)
        q_group = lax.dynamic_slice_in_dim(queries[which_resp], head_start, GQ, 1)
        grad_group = lax.dynamic_slice_in_dim(masked[which_resp], head_start, GQ, 1)
        key_rows = jnp.concatenate([prefix[:, which_head, 0], own_keys[which_resp, :, which_head]], 0)
        value_rows = jnp.concatenate([prefix[:, which_head, 1], own_values[which_resp, :, which_head]], 0)
        return one_group(q_group, key_rows, value_rows, grad_group)

    d_query, d_key, d_value = lax.map(one_pair, jnp.arange(RESP * KVH, dtype=jnp.int32))
    d_query = d_query.reshape(RESP, KVH, GQ, LEN, HD).transpose(0, 3, 1, 2, 4).reshape(RESP, LEN, QH, HD)
    d_key = d_key.reshape(RESP, KVH, PROMPT + LEN, HD)
    d_value = d_value.reshape(RESP, KVH, PROMPT + LEN, HD)
    prompt_dk = rotate(jnp.sum(d_key[:, :, :PROMPT], 0), cos_prompt[None], -sin_prompt[None])
    prompt_dv = jnp.sum(d_value[:, :, :PROMPT], 0)
    prompt_grad = jnp.stack([prompt_dk, prompt_dv], 1).transpose(2, 0, 1, 3).reshape(PROMPT, KVW).astype(jnp.bfloat16)
    d_hidden = jnp.dot(prompt_grad, w_kv.T, preferred_element_type=jnp.float32).astype(jnp.bfloat16)
    d_wkv = jnp.dot(prompt_hidden.T, prompt_grad, preferred_element_type=jnp.float32)
    d_q = rotate(d_query, cos_resp[None, :, None], -sin_resp[None, :, None]).astype(jnp.bfloat16).reshape(RESP, LEN, QH * HD)
    resp_dk = rotate(d_key[:, :, PROMPT:], cos_resp[None, None], -sin_resp[None, None])
    resp_dv = d_value[:, :, PROMPT:]
    d_kv_resp = jnp.stack([resp_dk, resp_dv], 2).transpose(0, 3, 1, 2, 4).reshape(RESP, LEN, KVW).astype(jnp.bfloat16)
    return (d_q, d_kv_resp, d_hidden, d_wkv)
```

```python
import functools

import jax
import jax.numpy as jnp
import numpy as np
from jax import lax
from jax.experimental import pallas as pl
from jax.experimental.pallas import tpu as pltpu
from jax.sharding import PartitionSpec as P

HD = 128
GQ = 8
THETA = 1000000.0
SCALE = HD**-0.5
MESH = pl.DeviceIdType.MESH
BF = jnp.bfloat16
F32 = jnp.float32


def tables(rows, groups):
    ladder = np.arange(HD // 2)
    frequency = (THETA ** (-2.0 * ladder / HD)).astype(np.float32).astype(np.float64)

    def both(positions):
        turned = positions[:, None] * frequency[None, :]
        cos, sin = np.cos(turned), np.sin(turned)
        return np.concatenate([cos, cos, -sin, sin], 1).astype(np.float32)

    return both(np.arange(rows)), both(np.arange(groups) * rows)


def dot(a, b):
    return lax.dot_general(a, b, (((1,), (0,)), ((), ())), preferred_element_type=F32)


def rotate(v, cos, sin):
    return v * cos + pltpu.roll(v, HD // 2, 1) * sin


def turned_tables(base_ref, start_ref, block):
    cos, sin = base_ref[:, :HD], base_ref[:, HD:]
    turn = start_ref[block]
    cos0, sin0 = turn[:, :HD], turn[:, HD:]
    return cos * cos0 - sin * sin0, sin * cos0 + cos * sin0


def kernel(
    nx, nt, x_ref, w_ref, q_ref, do_ref, kv_ref, len_ref, base_ref, start_ref,
    dq_ref, dkv_ref, dh_ref, dw_ref,
    q_rows, q_cols, g_rows, g_cols, kv, kv_t, e, top, low, delta, dq_t, cos_r, sin_r,
    b_send, b_recv, raw, x_t, grad_send, grad_recv, heads, cols, dh_acc,
    b_ss, b_rs, x_ss, x_rs, c_ss, c_rs, e_ss, e_rs, f_ss, f_rs, a_ss, a_rs,
):
    T = x_ref.shape[0]
    D = x_ref.shape[1]
    H = T // 2
    W2 = 2 * HD
    NG = 2 * nx
    half = nt // 2
    own = NG
    grp, tp, dp = lax.axis_index("grp"), lax.axis_index("tp"), lax.axis_index("dp")
    x, y = grp // 2, grp % 2

    def offset(k):
        j = k % 4
        return j + j // 2 - 2 * (j // 3), k // 4

    def peer(k):
        dx, dy = offset(k)
        return ((x + dx) % nx) * 2 + (y + dy) % 2

    def source(k):
        dx, dy = offset(k)
        return ((x - dx + nx) % nx) * 2 + (y + dy) % 2

    def on_grp(other):
        return (other, tp, dp)

    ring = [(grp, (tp + 1) % nt, dp), (grp, (tp + nt - 1) % nt, dp)]

    def remote(src, dst, ss, rs, device):
        return pltpu.make_async_remote_copy(
            src_ref=src, dst_ref=dst, send_sem=ss, recv_sem=rs, device_id=device, device_id_type=MESH
        )

    started = []

    def go(copy):
        copy.start()
        started.append(copy)

    barrier = pltpu.get_barrier_semaphore()
    for k in range(1, NG):
        pl.semaphore_signal(barrier, inc=1, device_id=on_grp(peer(k)), device_id_type=MESH)
    for device in ring:
        pl.semaphore_signal(barrier, inc=1, device_id=device, device_id_type=MESH)

    def part(h):
        at = pl.ds(pl.multiple_of(h * W2, W2), W2)
        return dot(x_ref[...], w_ref[:, at])

    def rows(d, c):
        return slice(0, H) if (d + c) % 2 == 0 else slice(H, T)

    def b_copy(d, s, c):
        return remote(b_send.at[d, s, c], b_recv.at[d, s, c], b_ss.at[d, s, c], b_rs.at[d, s, c], ring[d])

    def x_copy(src, dst, i, to):
        return remote(x_t.at[src], x_t.at[dst], x_ss.at[dst, i], x_rs.at[dst, i], on_grp(peer(to)))

    def x_half(src, dst, i, to):
        at = pl.ds(i * (D // 2), D // 2)
        return remote(
            x_t.at[src, at], x_t.at[dst, at], x_ss.at[dst, i], x_rs.at[dst, i], on_grp(peer(to))
        )

    far = part((tp + half) % nt)
    for d in range(2):
        b_send[d, 0, 0] = far[rows(d, 0)].astype(BF)
    x_t[0] = x_ref[...].astype(F32).T.astype(BF)
    pl.semaphore_wait(barrier, NG - 1 + 2)
    for d in range(2):
        go(b_copy(d, 0, 0))

    def prep_tables():
        c, s = turned_tables(base_ref, start_ref, NG)
        cos_r[...] = c
        sin_r[...] = s
        dq_t[...] = jnp.zeros_like(dq_t)

    def prep(c):
        def run():
            at = slice(c * HD, (c + 1) * HD)
            ct = slice(c * T, (c + 1) * T)
            live = lax.broadcasted_iota(jnp.int32, (T, HD), 0) < len_ref[0]
            qf = rotate(q_ref[:, at].astype(F32), cos_r[...], sin_r[...])
            q_rows[c] = qf.astype(BF)
            q_cols[:, ct] = qf.T.astype(BF)
            gf = jnp.where(live, do_ref[:, at].astype(F32), 0.0)
            g_rows[c] = gf.astype(BF)
            g_cols[:, ct] = gf.T.astype(BF)

        return run

    def prep_own():
        kv[own, :, :HD] = rotate(kv_ref[:, :HD].astype(F32), cos_r[...], sin_r[...]).astype(BF)
        kv[own, :, HD:] = kv_ref[:, HD:]

    def scores(p, is_own):
        kv_t[p] = kv[p].astype(F32).T.astype(BF)
        k = kv[p, :, :HD]
        if is_own:
            visible = lax.broadcasted_iota(jnp.int32, (T, T), 0) <= lax.broadcasted_iota(
                jnp.int32, (T, T), 1
            )
        for c in range(GQ):
            ct = slice(c * T, (c + 1) * T)
            s = dot(k, q_cols[:, ct]) * SCALE
            if is_own:
                s = jnp.where(visible, s, -jnp.inf)
            m = jnp.max(s, axis=0, keepdims=True)
            raised = jnp.exp(s - m)
            e[p, :, ct] = raised
            top[p, :, ct] = m
            low[p, :, ct] = jnp.sum(raised, axis=0, keepdims=True)

    fillers = [prep_tables] + [prep(c) for c in range(GQ)] + [prep_own]

    def fill(count):
        for _ in range(count):
            if fillers:
                fillers.pop(0)()

    for s in range(1, half):
        for d in range(2):
            sign = 1 if d == 0 else nt - 1
            raw[d] = part((tp + sign * (half - s)) % nt)
        for c in (1, 0):
            for d in range(2):
                v = raw[d, rows(d, c)]
                if c == 0 or s > 1:
                    b_copy(d, s - 1, c).wait_recv()
                    v = v + b_recv[d, s - 1, c].astype(F32)
                b_send[d, s, c] = v.astype(BF)
                go(b_copy(d, s, c))
            if s == 1 and c == 1:
                for k in (1, 2, 4):
                    go(x_copy(0, k, 0, k))
            fill(2)
    fill(len(fillers))
    raw[0] = part(tp)
    scores(own, True)
    for c in (1, 0):
        for d in range(2):
            if c == 0 or half > 1:
                b_copy(d, half - 1, c).wait_recv()
                raw[0, rows(d, c)] = raw[0, rows(d, c)] + b_recv[d, half - 1, c].astype(F32)
    cos_p, sin_p = turned_tables(base_ref, start_ref, grp)
    kv[0, :, :HD] = rotate(raw[0, :, :HD], cos_p, sin_p).astype(BF)
    kv[0, :, HD:] = raw[0, :, HD:].astype(BF)

    def c_copy(k):
        return remote(kv.at[0], kv.at[k], c_ss.at[k], c_rs.at[k], on_grp(peer(k)))

    for k in range(1, NG):
        go(c_copy(k))
    scores(0, False)

    def score_step(k, carry):
        c_copy(k).wait_recv()
        scores(k, False)
        return carry

    lax.fori_loop(1, NG, score_step, 0)
    for k in (1, 2, 4):
        x_copy(0, k, 0, k).wait_recv()
    go(x_half(1, 3, 0, 1))
    go(x_half(2, 3, 1, 2))
    go(x_copy(4, 5, 0, 1))
    go(x_copy(4, 6, 0, 2))

    m = functools.reduce(jnp.maximum, [top[p] for p in range(NG + 1)])
    weights = [jnp.exp(top[p] - m) for p in range(NG + 1)]
    total = functools.reduce(jnp.add, [weights[p] * low[p] for p in range(NG + 1)])
    inverse = 1.0 / total
    for p in range(NG + 1):
        top[p] = weights[p] * inverse
    for c in range(GQ):
        ct = slice(c * T, (c + 1) * T)
        acc = jnp.zeros((HD, T), F32)
        for p in range(NG + 1):
            acc = acc + dot(kv_t[p, HD:], (e[p, :, ct] * top[p, :, ct]).astype(BF))
        delta[:, ct] = jnp.sum(
            acc.astype(BF).astype(F32) * g_cols[:, ct].astype(F32), axis=0, keepdims=True
        )

    def backward(p):
        v = kv[p, :, HD:]
        dk = jnp.zeros((T, HD), F32)
        dv = jnp.zeros((T, HD), F32)
        for c in range(GQ):
            ct = slice(c * T, (c + 1) * T)
            a = e[p, :, ct] * top[p, :, ct]
            da = dot(v, g_cols[:, ct])
            ds = (a * (da - delta[:, ct])).astype(BF)
            dv = dv + dot(a.astype(BF), g_rows[c])
            dk = dk + dot(ds, q_rows[c])
            dq_t[:, ct] += dot(kv_t[p, :HD], ds)
        return dk * SCALE, dv

    def e_copy(k):
        return remote(
            grad_send.at[k], grad_recv.at[k], e_ss.at[k], e_rs.at[k], on_grp(source(k))
        )

    def grad_step(i, carry):
        k = NG - 1 - i
        dk, dv = backward(k)
        grad_send[k, :, :HD] = dk.astype(BF)
        grad_send[k, :, HD:] = dv.astype(BF)
        e_copy(k).start()
        return carry

    lax.fori_loop(0, 3, grad_step, 0)
    for k in (5, 6):
        x_copy(4, k, 0, 1).wait_recv()
    go(x_half(5, 7, 0, 1))
    go(x_half(6, 7, 1, 2))
    lax.fori_loop(3, NG - 1, grad_step, 0)
    dk, dv = backward(own)
    dkv_ref[:, :HD] = rotate(dk, cos_r[...], -sin_r[...]).astype(BF)
    dkv_ref[:, HD:] = dv.astype(BF)
    dk, dv = backward(0)
    raw[0, :, :HD] = dk
    raw[0, :, HD:] = dv

    def sum_step(i, carry):
        k = NG - 1 - i
        e_copy(k).wait_recv()
        raw[0] = raw[0] + grad_recv[k].astype(F32)
        return carry

    lax.fori_loop(0, NG - 1, sum_step, 0)
    cos_p, sin_p = turned_tables(base_ref, start_ref, grp)
    heads[0, :, :HD] = rotate(raw[0, :, :HD], cos_p, -sin_p).astype(BF)
    heads[0, :, HD:] = raw[0, :, HD:].astype(BF)

    def f_copy(d, s, c):
        src, dst = ((nt - s) % nt, nt - s - 1) if d == 0 else (s, s + 1)
        at = pl.ds(c * H, H)
        return remote(
            heads.at[src, at], heads.at[dst, at], f_ss.at[d, s, c], f_rs.at[d, s, c], ring[d]
        )

    def a_copy(slot):
        return remote(
            heads.at[slot], cols.at[grp], a_ss.at[slot], a_rs.at[grp], on_grp((tp + slot) % nt)
        )

    def pass_on(slot):
        @pl.when((tp + slot) % nt != grp)
        def _():
            a_copy(slot).start()

    def hidden(slot, first):
        h = (tp + slot) % nt
        at = pl.ds(pl.multiple_of(h * W2, W2), W2)
        term = lax.dot_general(
            heads[slot], w_ref[:, at], (((1,), (1,)), ((), ())), preferred_element_type=F32
        )
        if first:
            dh_acc[...] = term
        else:
            dh_acc[...] += term

    def query_out(c):
        ct = slice(c * T, (c + 1) * T)
        v = dq_t[:, ct].T * SCALE
        dq_ref[:, c * HD : (c + 1) * HD] = rotate(v, cos_r[...], -sin_r[...]).astype(BF)

    for c in range(2):
        for d in range(2):
            if half > 1 or c == d:
                go(f_copy(d, 0, c))
    pass_on(0)
    hidden(0, True)
    for c in range(4):
        query_out(c)
    for s in range(1, half):
        for c in range(2):
            for d in range(2):
                f_copy(d, s - 1, c).wait_recv()
                if s < half - 1 or c == d:
                    go(f_copy(d, s, c))
        for slot in (nt - s, s):
            pass_on(slot)
            hidden(slot, False)
        if s == 1:
            for c in range(4, GQ):
                query_out(c)
    f_copy(0, half - 1, 0).wait_recv()
    f_copy(1, half - 1, 1).wait_recv()
    pass_on(half)
    hidden(half, False)
    dh_ref[...] = dh_acc[...].astype(BF)

    for i in range(2):
        x_half(1, 3, i, 1).wait_recv()
        x_half(1, 7, i, 1).wait_recv()
    dw_ref[...] = dot(x_t[0], heads[(grp - tp + nt) % nt])

    def weight_step(k, carry):
        other = source(k)
        remote(
            heads.at[0], cols.at[other], a_ss.at[0], a_rs.at[other], on_grp(peer(1))
        ).wait_recv()
        dw_ref[...] += dot(x_t[k], cols[other])
        return carry

    lax.fori_loop(1, NG, weight_step, 0)

    for copy in started:
        copy.wait_send()

    def end_step(k, carry):
        e_copy(k).wait_send()
        return carry

    lax.fori_loop(1, NG, end_step, 0)
    for slot in range(nt):

        @pl.when((tp + slot) % nt != grp)
        def _():
            a_copy(slot).wait_send()


def local(nx, nt, prompt_hidden, w_kv, resp_q, resp_kv, d_out, lengths):
    T, D = prompt_hidden.shape
    NG = 2 * nx
    W2 = 2 * HD
    base, start = tables(T, NG + 1)
    start = start[:, None]
    vm = pl.BlockSpec(memory_space=pltpu.VMEM)
    dma = pltpu.SemaphoreType.DMA
    half = nt // 2
    dq, dkv, dh, dw = pl.pallas_call(
        functools.partial(kernel, nx, nt),
        out_shape=(
            jax.ShapeDtypeStruct((T, GQ * HD), BF),
            jax.ShapeDtypeStruct((T, W2), BF),
            jax.ShapeDtypeStruct((T, D), BF),
            jax.ShapeDtypeStruct((D, W2), F32),
        ),
        in_specs=[vm] * 5 + [pl.BlockSpec(memory_space=pltpu.SMEM)] + [vm] * 2,
        out_specs=(vm,) * 4,
        scratch_shapes=[
            pltpu.VMEM((GQ, T, HD), BF),
            pltpu.VMEM((HD, GQ * T), BF),
            pltpu.VMEM((GQ, T, HD), BF),
            pltpu.VMEM((HD, GQ * T), BF),
            pltpu.VMEM((NG + 1, T, W2), BF),
            pltpu.VMEM((NG + 1, W2, T), BF),
            pltpu.VMEM((NG + 1, T, GQ * T), F32),
            pltpu.VMEM((NG + 1, 1, GQ * T), F32),
            pltpu.VMEM((NG + 1, 1, GQ * T), F32),
            pltpu.VMEM((1, GQ * T), F32),
            pltpu.VMEM((HD, GQ * T), F32),
            pltpu.VMEM((T, HD), F32),
            pltpu.VMEM((T, HD), F32),
            pltpu.VMEM((2, half, 2, T // 2, W2), BF),
            pltpu.VMEM((2, half, 2, T // 2, W2), BF),
            pltpu.VMEM((2, T, W2), F32),
            pltpu.VMEM((NG, D, T), BF),
            pltpu.VMEM((NG, T, W2), BF),
            pltpu.VMEM((NG, T, W2), BF),
            pltpu.VMEM((nt, T, W2), BF),
            pltpu.VMEM((NG, T, W2), BF),
            pltpu.VMEM((T, D), F32),
            dma((2, half, 2)),
            dma((2, half, 2)),
            dma((NG, 2)),
            dma((NG, 2)),
            dma((NG,)),
            dma((NG,)),
            dma((NG,)),
            dma((NG,)),
            dma((2, half, 2)),
            dma((2, half, 2)),
            dma((nt,)),
            dma((NG,)),
        ],
        compiler_params=pltpu.CompilerParams(
            collective_id=0, has_side_effects=True, vmem_limit_bytes=60 * 2**20
        ),
        name="prefix_attention_backward",
    )(
        prompt_hidden,
        w_kv,
        resp_q.reshape(T, GQ * HD),
        d_out.reshape(T, GQ * HD),
        resp_kv.reshape(T, W2),
        lengths,
        jnp.asarray(base),
        jnp.asarray(start),
    )
    return dq[None], dkv[None], dh, dw


def solution(mesh):
    nx = mesh.shape["grp"] // 2
    nt = mesh.shape["tp"]
    return jax.shard_map(
        functools.partial(local, nx, nt),
        mesh=mesh,
        in_specs=(
            P(("dp", "grp"), "tp"),
            P("tp", None),
            P(("dp", "grp"), None, "tp"),
            P(("dp", "grp"), None, "tp"),
            P(("dp", "grp"), None, "tp"),
            P(("dp", "grp")),
        ),
        out_specs=(
            P(("dp", "grp"), None, "tp"),
            P(("dp", "grp"), None, "tp"),
            P(("dp", "grp"), "tp"),
            P(("dp", "tp"), "grp"),
        ),
        check_vma=False,
    )
```

```python
import functools

import jax
import jax.numpy as jnp
import numpy as np
from jax import lax
from jax.experimental import pallas as pl
from jax.experimental.pallas import tpu as pltpu
from jax.sharding import PartitionSpec as P

HD = 128
GQ = 8
THETA = 1000000.0
SCALE = HD**-0.5
MESH = pl.DeviceIdType.MESH
BF = jnp.bfloat16
F32 = jnp.float32


def tables(rows, groups):
    ladder = np.arange(HD // 2)
    frequency = (THETA ** (-2.0 * ladder / HD)).astype(np.float32).astype(np.float64)

    def both(positions):
        turned = positions[:, None] * frequency[None, :]
        cos, sin = np.cos(turned), np.sin(turned)
        return np.concatenate([cos, cos, -sin, sin], 1).astype(np.float32)

    return both(np.arange(rows)), both(np.arange(groups) * rows)


def dot(a, b):
    return lax.dot_general(a, b, (((1,), (0,)), ((), ())), preferred_element_type=F32)


def rotate(v, cos, sin):
    return v * cos + pltpu.roll(v, HD // 2, 1) * sin


def turned_tables(base_ref, start_ref, block):
    cos, sin = base_ref[:, :HD], base_ref[:, HD:]
    turn = start_ref[block]
    cos0, sin0 = turn[:, :HD], turn[:, HD:]
    return cos * cos0 - sin * sin0, sin * cos0 + cos * sin0


def kernel(
    nx, nt, x_ref, w_ref, q_ref, do_ref, kv_ref, len_ref, base_ref, start_ref,
    dq_ref, dkv_ref, dh_ref, dw_ref,
    q_rows, q_cols, g_rows, g_cols, kb, vb, kt, vt, e, top, low, delta, ds_all, o_t, cos_r, sin_r,
    b_send, b_recv, raw, mine, x_t, grad_send, grad_recv, heads, cols, dh_acc,
    b_ss, b_rs, x_ss, x_rs, c_ss, c_rs, e_ss, e_rs, f_ss, f_rs, a_ss, a_rs,
):
    T = x_ref.shape[0]
    D = x_ref.shape[1]
    H = T // 2
    W2 = 2 * HD
    NG = 2 * nx
    own = NG
    kv = (kb, vb)
    grp, tp, dp = lax.axis_index("grp"), lax.axis_index("tp"), lax.axis_index("dp")
    x, y = grp // 2, grp % 2

    def offset(k):
        j = k % 4
        return j + j // 2 - 2 * (j // 3), k // 4

    def peer(k):
        dx, dy = offset(k)
        return ((x + dx) % nx) * 2 + (y + dy) % 2

    def source(k):
        dx, dy = offset(k)
        return ((x - dx + nx) % nx) * 2 + (y + dy) % 2

    def on_grp(other):
        return (other, tp, dp)

    def on_tp(step):
        return (grp, (tp + step + nt) % nt, dp)

    def remote(src, dst, ss, rs, device):
        return pltpu.make_async_remote_copy(
            src_ref=src, dst_ref=dst, send_sem=ss, recv_sem=rs, device_id=device, device_id_type=MESH
        )

    started = []

    def go(copy):
        copy.start()
        started.append(copy)

    barrier = pltpu.get_barrier_semaphore()
    for k in range(1, NG):
        pl.semaphore_signal(barrier, inc=1, device_id=on_grp(peer(k)), device_id_type=MESH)
    for step in range(1, nt):
        pl.semaphore_signal(barrier, inc=1, device_id=on_tp(step), device_id_type=MESH)

    def part(h, u):
        at = pl.ds(pl.multiple_of(h * W2 + u * HD, HD), HD)
        return dot(x_ref[...], w_ref[:, at])

    def b_copy(u, d, i):
        step = (2, 1, 1, 2)[i]
        at = pl.ds(d * H, H) if i == 0 else pl.ds(0, T)
        return remote(
            b_send.at[u, d, i, at], b_recv.at[u, d, i, at], b_ss.at[u, d, i], b_rs.at[u, d, i],
            on_tp(step if d == 0 else -step),
        )

    def x_copy(src, dst, i, to):
        return remote(x_t.at[src], x_t.at[dst], x_ss.at[dst, i], x_rs.at[dst, i], on_grp(peer(to)))

    def x_half(src, dst, i, to):
        at = pl.ds(i * (D // 2), D // 2)
        return remote(
            x_t.at[src, at], x_t.at[dst, at], x_ss.at[dst, i], x_rs.at[dst, i], on_grp(peer(to))
        )

    def sum_first(u):
        far = part((tp + 4) % nt, u).astype(BF)
        for d in range(2):
            b_send[u, d, 0, d * H : (d + 1) * H] = far[d * H : (d + 1) * H]
            b_send[u, d, 1] = part((tp + (3 if d == 0 else nt - 3)) % nt, u).astype(BF)

    def sum_send(u):
        for i in range(2):
            for d in range(2):
                go(b_copy(u, d, i))

    def sum_near(u):
        for d in range(2):
            b_send[u, d, 2] = part((tp + (1 if d == 0 else nt - 1)) % nt, u).astype(BF)
            go(b_copy(u, d, 2))
        for d in range(2):
            raw[u, d] = part((tp + (2 if d == 0 else nt - 2)) % nt, u)
        mine[u] = part(tp, u)

    def sum_second(u):
        for d in range(2):
            at = slice(d * H, (d + 1) * H)
            b_copy(u, d, 0).wait_recv()
            raw[u, d, at] = raw[u, d, at] + b_recv[u, d, 0, at].astype(F32)
            b_copy(u, d, 1).wait_recv()
            b_send[u, d, 3] = (raw[u, d] + b_recv[u, d, 1].astype(F32)).astype(BF)
            go(b_copy(u, d, 3))

    def sum_end(u):
        total = mine[u]
        for i in (2, 3):
            for d in range(2):
                b_copy(u, d, i).wait_recv()
                total = total + b_recv[u, d, i].astype(F32)
        mine[u] = total

    def c_copy(u, k):
        return remote(kv[u].at[0], kv[u].at[k], c_ss.at[u, k], c_rs.at[u, k], on_grp(peer(k)))

    sum_first(0)
    x_t[0] = x_ref[...].astype(F32).T.astype(BF)
    pl.semaphore_wait(barrier, NG - 1 + nt - 1)
    sum_send(0)
    sum_near(0)
    for k in (1, 2, 4):
        go(x_copy(0, k, 0, k))

    def prep_tables():
        c, s = turned_tables(base_ref, start_ref, NG)
        cos_r[...] = c
        sin_r[...] = s
        o_t[...] = jnp.zeros_like(o_t)

    def prep(c):
        def run():
            at = slice(c * HD, (c + 1) * HD)
            ct = slice(c * T, (c + 1) * T)
            live = lax.broadcasted_iota(jnp.int32, (T, HD), 0) < len_ref[0]
            qf = rotate(q_ref[:, at].astype(F32), cos_r[...], sin_r[...])
            q_rows[c] = qf.astype(BF)
            q_cols[:, ct] = qf.T.astype(BF)
            gf = jnp.where(live, do_ref[:, at].astype(F32), 0.0)
            g_rows[c] = gf.astype(BF)
            g_cols[:, ct] = gf.T.astype(BF)

        return run

    def prep_own():
        kb[own] = rotate(kv_ref[:, :HD].astype(F32), cos_r[...], sin_r[...]).astype(BF)
        vb[own] = kv_ref[:, HD:]

    def scores(p, is_own):
        kt[p] = kb[p].astype(F32).T.astype(BF)
        k = kb[p]
        if is_own:
            visible = lax.broadcasted_iota(jnp.int32, (T, T), 0) <= lax.broadcasted_iota(
                jnp.int32, (T, T), 1
            )
        for c in range(GQ):
            ct = slice(c * T, (c + 1) * T)
            s = dot(k, q_cols[:, ct]) * SCALE
            if is_own:
                s = jnp.where(visible, s, -jnp.inf)
            m = jnp.max(s, axis=0, keepdims=True)
            raised = jnp.exp(s - m)
            e[p, :, ct] = raised
            top[p, :, ct] = m
            low[p, :, ct] = jnp.sum(raised, axis=0, keepdims=True)

    fillers = [prep_tables] + [prep(c) for c in range(GQ)] + [prep_own]

    def fill(count):
        for _ in range(count):
            if fillers:
                fillers.pop(0)()

    fill(4)
    sum_second(0)
    sum_first(1)
    sum_send(1)
    sum_near(1)
    fill(len(fillers))
    scores(own, True)
    sum_end(0)
    cos_p, sin_p = turned_tables(base_ref, start_ref, grp)
    kb[0] = rotate(mine[0], cos_p, sin_p).astype(BF)
    for k in range(1, NG):
        go(c_copy(0, k))
    sum_second(1)
    scores(0, False)
    for k in (1, 2):
        x_copy(0, k, 0, k).wait_recv()
    go(x_half(1, 3, 0, 1))
    go(x_half(2, 3, 1, 2))

    def score_step(k, carry):
        c_copy(0, k).wait_recv()
        scores(k, False)
        return carry

    lax.fori_loop(1, 3, score_step, 0)
    sum_end(1)
    vb[0] = mine[1].astype(BF)
    for k in range(1, NG):
        go(c_copy(1, k))
    lax.fori_loop(3, NG, score_step, 0)
    x_copy(0, 4, 0, 4).wait_recv()
    go(x_copy(4, 5, 0, 1))
    go(x_copy(4, 6, 0, 2))

    m = functools.reduce(jnp.maximum, [top[p] for p in range(NG + 1)])
    weights = [jnp.exp(top[p] - m) for p in range(NG + 1)]
    total = functools.reduce(jnp.add, [weights[p] * low[p] for p in range(NG + 1)])
    inverse = 1.0 / total
    for p in range(NG + 1):
        top[p] = weights[p] * inverse

    def e_copy(u, k):
        return remote(
            grad_send.at[u, k], grad_recv.at[u, k], e_ss.at[u, k], e_rs.at[u, k], on_grp(source(k))
        )

    def weigh(p):
        vt[p] = vb[p].astype(F32).T.astype(BF)
        dv = jnp.zeros((T, HD), F32)
        for c in range(GQ):
            ct = slice(c * T, (c + 1) * T)
            ab = (e[p, :, ct] * top[p, :, ct]).astype(BF)
            o_t[:, ct] += dot(vt[p], ab)
            dv = dv + dot(ab, g_rows[c])
        return dv

    def weigh_step(k, carry):
        c_copy(1, k).wait_recv()
        grad_send[1, k] = weigh(k).astype(BF)
        e_copy(1, k).start()
        return carry

    dkv_ref[:, HD:] = weigh(own).astype(BF)
    lax.fori_loop(1, NG, weigh_step, 0)
    mine[1] = weigh(0)
    for c in range(GQ):
        ct = slice(c * T, (c + 1) * T)
        delta[:, ct] = jnp.sum(
            o_t[:, ct].astype(BF).astype(F32) * g_cols[:, ct].astype(F32), axis=0, keepdims=True
        )

    def backward(p):
        v = vb[p]
        dk = jnp.zeros((T, HD), F32)
        for c in range(GQ):
            ct = slice(c * T, (c + 1) * T)
            a = e[p, :, ct] * top[p, :, ct]
            da = dot(v, g_cols[:, ct])
            ds = (a * (da - delta[:, ct])).astype(BF)
            ds_all[p, :, ct] = ds
            dk = dk + dot(ds, q_rows[c])
        return dk * SCALE

    def grad_step(i, carry):
        k = NG - 1 - i
        grad_send[0, k] = backward(k).astype(BF)
        e_copy(0, k).start()
        return carry

    def gather_sum(u):
        def step(i, carry):
            k = 1 + i if u == 1 else NG - 1 - i
            e_copy(u, k).wait_recv()
            mine[u] = mine[u] + grad_recv[u, k].astype(F32)
            return carry

        lax.fori_loop(0, NG - 1, step, 0)

    def v_copy(step):
        return remote(
            heads.at[1, 0], heads.at[1, nt - step], f_ss.at[1, step], f_rs.at[1, step], on_tp(step)
        )

    def k_copy(d, i):
        at = pl.ds(d * H, H) if i == 3 else pl.ds(0, T)
        step = (1, 2, 1, 2)[i]
        src = (0, 0, 2, 2)[i]
        dst = (1, 2, 3, 4)[i]
        if d == 0:
            src, dst = (nt - src) % nt, nt - dst
        return remote(
            heads.at[0, src, at], heads.at[0, dst, at], f_ss.at[0, d * 4 + i], f_rs.at[0, d * 4 + i],
            on_tp(step if d == 0 else -step),
        )

    def a_copy(u, slot):
        return remote(
            heads.at[u, slot], cols.at[u, grp], a_ss.at[u, slot], a_rs.at[u, grp], on_grp((tp + slot) % nt)
        )

    def pass_on(u, slot):
        @pl.when((tp + slot) % nt != grp)
        def _():
            a_copy(u, slot).start()

    def hidden(u, slot, first=False):
        h = (tp + slot) % nt
        at = pl.ds(pl.multiple_of(h * W2 + u * HD, HD), HD)
        term = lax.dot_general(
            heads[u, slot], w_ref[:, at], (((1,), (1,)), ((), ())), preferred_element_type=F32
        )
        if first:
            dh_acc[...] = term
        else:
            dh_acc[...] += term

    def query_out(c):
        ct = slice(c * T, (c + 1) * T)
        dq = jnp.zeros((HD, T), F32)
        for p in range(NG + 1):
            dq = dq + dot(kt[p], ds_all[p, :, ct])
        dq_ref[:, c * HD : (c + 1) * HD] = rotate(dq.T * SCALE, cos_r[...], -sin_r[...]).astype(BF)

    lax.fori_loop(0, 2, grad_step, 0)
    gather_sum(1)
    heads[1, 0] = mine[1].astype(BF)
    for step in (1, nt - 1, 2, nt - 2, 3, nt - 3, 4):
        go(v_copy(step))
    pass_on(1, 0)
    lax.fori_loop(2, 5, grad_step, 0)
    for k in (5, 6):
        x_copy(4, k, 0, 1).wait_recv()
    go(x_half(5, 7, 0, 1))
    go(x_half(6, 7, 1, 2))
    lax.fori_loop(5, NG - 1, grad_step, 0)
    mine[0] = backward(0)
    gather_sum(0)
    cos_p, sin_p = turned_tables(base_ref, start_ref, grp)
    heads[0, 0] = rotate(mine[0], cos_p, -sin_p).astype(BF)
    for i in (1, 0):
        for d in range(2):
            go(k_copy(d, i))
    pass_on(0, 0)
    for step in (1, nt - 1, 2, nt - 2, 3, nt - 3, 4):
        v_copy(step).wait_recv()
        pass_on(1, nt - step)
    dk = backward(own)
    dkv_ref[:, :HD] = rotate(dk, cos_r[...], -sin_r[...]).astype(BF)
    for d in range(2):
        k_copy(d, 1).wait_recv()
        for i in (2, 3):
            go(k_copy(d, i))
    for i in (1, 0):
        for d in range(2):
            if i == 0:
                k_copy(d, i).wait_recv()
            pass_on(0, nt - i - 1 if d == 0 else i + 1)
    for c in range(4):
        query_out(c)
    for d in range(2):
        k_copy(d, 2).wait_recv()
        pass_on(0, nt - 3 if d == 0 else 3)
    for d in range(2):
        k_copy(d, 3).wait_recv()
    pass_on(0, 4)
    for c in range(4, GQ):
        query_out(c)
    hidden(1, 0, True)
    for slot in range(1, nt):
        hidden(1, slot)
    for slot in range(nt):
        hidden(0, slot)

    def x_end():
        for i in range(2):
            x_half(1, 3, i, 1).wait_recv()
            x_half(1, 7, i, 1).wait_recv()

    def weight_step(u):
        def step(k, carry):
            other = source(k)
            remote(
                heads.at[u, 0], cols.at[u, other], a_ss.at[u, 0], a_rs.at[u, other], on_grp(peer(1))
            ).wait_recv()
            dw_ref[:, u * HD : (u + 1) * HD] += dot(x_t[k], cols[u, other])
            return carry

        return step

    dh_ref[...] = dh_acc[...].astype(BF)
    x_end()
    dw_ref[:, HD:] = dot(x_t[0], heads[1, (grp - tp + nt) % nt])
    lax.fori_loop(1, NG, weight_step(1), 0)
    dw_ref[:, :HD] = dot(x_t[0], heads[0, (grp - tp + nt) % nt])
    lax.fori_loop(1, NG, weight_step(0), 0)

    for copy in started:
        copy.wait_send()

    def end_step(k, carry):
        e_copy(0, k).wait_send()
        e_copy(1, k).wait_send()
        return carry

    lax.fori_loop(1, NG, end_step, 0)
    for slot in range(nt):

        @pl.when((tp + slot) % nt != grp)
        def _():
            a_copy(0, slot).wait_send()
            a_copy(1, slot).wait_send()


def hand_over(*refs):
    n = len(refs) // 2
    for i in range(n):
        refs[n + i][...] = refs[i][...]


def local(nx, nt, prompt_hidden, w_kv, resp_q, resp_kv, d_out, lengths):
    T, D = prompt_hidden.shape
    NG = 2 * nx
    W2 = 2 * HD
    base, start = tables(T, NG + 1)
    start = start[:, None]
    vm = pl.BlockSpec(memory_space=pltpu.VMEM)
    dma = pltpu.SemaphoreType.DMA
    results = pl.pallas_call(
        functools.partial(kernel, nx, nt),
        out_shape=(
            jax.ShapeDtypeStruct((T, GQ * HD), BF),
            jax.ShapeDtypeStruct((T, W2), BF),
            jax.ShapeDtypeStruct((T, D), BF),
            jax.ShapeDtypeStruct((D, W2), F32),
        ),
        in_specs=[vm] * 5 + [pl.BlockSpec(memory_space=pltpu.SMEM)] + [vm] * 2,
        out_specs=(vm,) * 4,
        scratch_shapes=[
            pltpu.VMEM((GQ, T, HD), BF),
            pltpu.VMEM((HD, GQ * T), BF),
            pltpu.VMEM((GQ, T, HD), BF),
            pltpu.VMEM((HD, GQ * T), BF),
            pltpu.VMEM((NG + 1, T, HD), BF),
            pltpu.VMEM((NG + 1, T, HD), BF),
            pltpu.VMEM((NG + 1, HD, T), BF),
            pltpu.VMEM((NG + 1, HD, T), BF),
            pltpu.VMEM((NG + 1, T, GQ * T), F32),
            pltpu.VMEM((NG + 1, 1, GQ * T), F32),
            pltpu.VMEM((NG + 1, 1, GQ * T), F32),
            pltpu.VMEM((1, GQ * T), F32),
            pltpu.VMEM((NG + 1, T, GQ * T), BF),
            pltpu.VMEM((HD, GQ * T), F32),
            pltpu.VMEM((T, HD), F32),
            pltpu.VMEM((T, HD), F32),
            pltpu.VMEM((2, 2, 4, T, HD), BF),
            pltpu.VMEM((2, 2, 4, T, HD), BF),
            pltpu.VMEM((2, 2, T, HD), F32),
            pltpu.VMEM((2, T, HD), F32),
            pltpu.VMEM((NG, D, T), BF),
            pltpu.VMEM((2, NG, T, HD), BF),
            pltpu.VMEM((2, NG, T, HD), BF),
            pltpu.VMEM((2, nt, T, HD), BF),
            pltpu.VMEM((2, NG, T, HD), BF),
            pltpu.VMEM((T, D), F32),
            dma((2, 2, 4)),
            dma((2, 2, 4)),
            dma((NG, 2)),
            dma((NG, 2)),
            dma((2, NG)),
            dma((2, NG)),
            dma((2, NG)),
            dma((2, NG)),
            dma((2, nt)),
            dma((2, nt)),
            dma((2, nt)),
            dma((2, NG)),
        ],
        compiler_params=pltpu.CompilerParams(
            collective_id=0, has_side_effects=True, vmem_limit_bytes=60 * 2**20
        ),
        name="prefix_attention_backward",
    )(
        prompt_hidden,
        w_kv,
        resp_q.reshape(T, GQ * HD),
        d_out.reshape(T, GQ * HD),
        resp_kv.reshape(T, W2),
        lengths,
        jnp.asarray(base),
        jnp.asarray(start),
    )
    dq, dkv, dh, dw = pl.pallas_call(
        hand_over,
        out_shape=tuple(jax.ShapeDtypeStruct(r.shape, r.dtype) for r in results),
        in_specs=[vm] * 4,
        out_specs=(vm,) * 4,
        name="hand_over",
    )(*results)
    return dq[None], dkv[None], dh, dw


def solution(mesh):
    nx = mesh.shape["grp"] // 2
    nt = mesh.shape["tp"]
    return jax.shard_map(
        functools.partial(local, nx, nt),
        mesh=mesh,
        in_specs=(
            P(("dp", "grp"), "tp"),
            P("tp", None),
            P(("dp", "grp"), None, "tp"),
            P(("dp", "grp"), None, "tp"),
            P(("dp", "grp"), None, "tp"),
            P(("dp", "grp")),
        ),
        out_specs=(
            P(("dp", "grp"), None, "tp"),
            P(("dp", "grp"), None, "tp"),
            P(("dp", "grp"), "tp"),
            P(("dp", "tp"), "grp"),
        ),
        check_vma=False,
    )
```

```python
import functools

import jax
import jax.numpy as jnp
import numpy as np
from jax import lax
from jax.experimental import pallas as pl
from jax.experimental.pallas import tpu as pltpu
from jax.sharding import PartitionSpec as P

HD = 128
GQ = 8
THETA = 1000000.0
SCALE = HD**-0.5
SCALE2 = SCALE * float(np.log2(np.e))
MESH = pl.DeviceIdType.MESH
BF = jnp.bfloat16
F32 = jnp.float32


def tables(rows, groups):
    ladder = np.arange(HD // 2)
    frequency = (THETA ** (-2.0 * ladder / HD)).astype(np.float32).astype(np.float64)

    def both(positions):
        turned = positions[:, None] * frequency[None, :]
        cos, sin = np.cos(turned), np.sin(turned)
        return np.concatenate([cos, cos, -sin, sin], 1).astype(np.float32)

    return both(np.arange(rows)), both(np.arange(groups) * rows)


def dot(a, b):
    return lax.dot_general(a, b, (((1,), (0,)), ((), ())), preferred_element_type=F32)


def rotate(v, cos, sin):
    return v * cos + pltpu.roll(v, HD // 2, 1) * sin


def turned_tables(base_ref, start_ref, block):
    cos, sin = base_ref[:, :HD], base_ref[:, HD:]
    turn = start_ref[block]
    cos0, sin0 = turn[:, :HD], turn[:, HD:]
    return cos * cos0 - sin * sin0, sin * cos0 + cos * sin0


def kernel(
    nx, nt, x_in, w_in, q_in, do_in, kv_in, len_ref, base_in, start_ref,
    dq_out, dkv_out, dh_out, dw_out,
    x_ref, w_ref, q_ref, do_ref, kv_ref, base_ref, dq_ref, dkv_ref, dh_ref, dw_ref,
    q_rows, q_cols, g_rows, g_cols, kb, vb, kt, vt, e, top, low, delta, ds_all, cos_r, sin_r,
    b_send, b_recv, raw, mine, x_t, grad_send, grad_recv, heads, cols, dh_acc,
    b_ss, b_rs, x_ss, x_rs, c_ss, c_rs, e_ss, e_rs, f_ss, f_rs, a_ss, a_rs, in_sems, out_sems,
):
    T = x_ref.shape[0]
    D = x_ref.shape[1]
    H = T // 2
    W2 = 2 * HD
    NG = 2 * nx
    own = NG
    kv = (kb, vb)
    grp, tp, dp = lax.axis_index("grp"), lax.axis_index("tp"), lax.axis_index("dp")
    x, y = grp // 2, grp % 2

    def offset(k):
        j = k % 4
        return j + j // 2 - 2 * (j // 3), k // 4

    def peer(k):
        dx, dy = offset(k)
        return ((x + dx) % nx) * 2 + (y + dy) % 2

    def source(k):
        dx, dy = offset(k)
        return ((x - dx + nx) % nx) * 2 + (y + dy) % 2

    def on_grp(other):
        return (other, tp, dp)

    def on_tp(step):
        return (grp, (tp + step + nt) % nt, dp)

    def remote(src, dst, ss, rs, device):
        return pltpu.make_async_remote_copy(
            src_ref=src, dst_ref=dst, send_sem=ss, recv_sem=rs, device_id=device, device_id_type=MESH
        )

    started = []

    def go(copy):
        copy.start()
        started.append(copy)

    barrier = pltpu.get_barrier_semaphore()
    for k in range(1, NG):
        pl.semaphore_signal(barrier, inc=1, device_id=on_grp(peer(k)), device_id_type=MESH)
    for step in range(1, nt):
        pl.semaphore_signal(barrier, inc=1, device_id=on_tp(step), device_id_type=MESH)

    loads = [
        pltpu.make_async_copy(src, dst, in_sems.at[i])
        for i, (src, dst) in enumerate(
            [(x_in, x_ref), (w_in, w_ref), (base_in, base_ref), (q_in, q_ref), (do_in, do_ref), (kv_in, kv_ref)]
        )
    ]
    for load in loads:
        load.start()

    def part(h, u):
        at = pl.ds(pl.multiple_of(h * W2 + u * HD, HD), HD)
        return dot(x_ref[...], w_ref[:, at])

    def b_copy(u, d, i):
        step = (2, 1, 1, 2)[i]
        at = pl.ds(d * H, H) if i == 0 else pl.ds(0, T)
        return remote(
            b_send.at[u, d, i, at], b_recv.at[u, d, i, at], b_ss.at[u, d, i], b_rs.at[u, d, i],
            on_tp(step if d == 0 else -step),
        )

    def x_copy(src, dst, i, to):
        return remote(x_t.at[src], x_t.at[dst], x_ss.at[dst, i], x_rs.at[dst, i], on_grp(peer(to)))

    def x_half(src, dst, i, to):
        at = pl.ds(i * (D // 2), D // 2)
        return remote(
            x_t.at[src, at], x_t.at[dst, at], x_ss.at[dst, i], x_rs.at[dst, i], on_grp(peer(to))
        )

    def sum_first(u):
        far = part((tp + 4) % nt, u).astype(BF)
        for d in range(2):
            b_send[u, d, 0, d * H : (d + 1) * H] = far[d * H : (d + 1) * H]
            b_send[u, d, 1] = part((tp + (3 if d == 0 else nt - 3)) % nt, u).astype(BF)

    def sum_send(u):
        for i in range(2):
            for d in range(2):
                go(b_copy(u, d, i))

    def sum_near(u):
        for d in range(2):
            b_send[u, d, 2] = part((tp + (1 if d == 0 else nt - 1)) % nt, u).astype(BF)
            go(b_copy(u, d, 2))
        for d in range(2):
            raw[u, d] = part((tp + (2 if d == 0 else nt - 2)) % nt, u)
        mine[u] = part(tp, u)

    def sum_second(u):
        for d in range(2):
            at = slice(d * H, (d + 1) * H)
            b_copy(u, d, 0).wait_recv()
            raw[u, d, at] = raw[u, d, at] + b_recv[u, d, 0, at].astype(F32)
            b_copy(u, d, 1).wait_recv()
            b_send[u, d, 3] = (raw[u, d] + b_recv[u, d, 1].astype(F32)).astype(BF)
            go(b_copy(u, d, 3))

    def sum_end(u):
        total = mine[u]
        for i in (2, 3):
            for d in range(2):
                b_copy(u, d, i).wait_recv()
                total = total + b_recv[u, d, i].astype(F32)
        mine[u] = total

    def c_copy(u, k):
        return remote(kv[u].at[0], kv[u].at[k], c_ss.at[u, k], c_rs.at[u, k], on_grp(peer(k)))

    loads[0].wait()
    x_t[0] = x_ref[...].astype(F32).T.astype(BF)
    loads[1].wait()
    sum_first(0)
    pl.semaphore_wait(barrier, NG - 1 + nt - 1)
    sum_send(0)
    sum_near(0)
    for k in (1, 2, 4):
        go(x_copy(0, k, 0, k))

    def prep_tables():
        c, s = turned_tables(base_ref, start_ref, NG)
        cos_r[...] = c
        sin_r[...] = s

    def prep(c):
        def run():
            at = slice(c * HD, (c + 1) * HD)
            ct = slice(c * T, (c + 1) * T)
            live = lax.broadcasted_iota(jnp.int32, (T, HD), 0) < len_ref[0]
            qf = rotate(q_ref[:, at].astype(F32), cos_r[...], sin_r[...])
            q_rows[c] = qf.astype(BF)
            q_cols[:, ct] = qf.T.astype(BF)
            gf = jnp.where(live, do_ref[:, at].astype(F32), 0.0)
            g_rows[c] = gf.astype(BF)
            g_cols[:, ct] = gf.T.astype(BF)

        return run

    def prep_own():
        kb[own] = rotate(kv_ref[:, :HD].astype(F32), cos_r[...], sin_r[...]).astype(BF)
        vb[own] = kv_ref[:, HD:]

    def scores(p, is_own):
        kt[p] = kb[p].astype(F32).T.astype(BF)
        k = kb[p]
        if is_own:
            visible = lax.broadcasted_iota(jnp.int32, (T, T), 0) <= lax.broadcasted_iota(
                jnp.int32, (T, T), 1
            )
        for c in range(GQ):
            ct = slice(c * T, (c + 1) * T)
            s = dot(k, q_cols[:, ct])
            if is_own:
                s = jnp.where(visible, s, -jnp.inf)
            m = jnp.max(s, axis=0, keepdims=True) * SCALE2
            raised = jnp.exp2(s * SCALE2 - m)
            e[p, :, ct] = raised
            top[p, :, ct] = m
            low[p, :, ct] = jnp.sum(raised, axis=0, keepdims=True)

    fillers = [prep_tables] + [prep(c) for c in range(GQ)] + [prep_own]

    def fill(count):
        for _ in range(count):
            if fillers:
                fillers.pop(0)()

    for load in loads[2:]:
        load.wait()
    fill(4)
    sum_second(0)
    sum_first(1)
    sum_send(1)
    sum_near(1)
    fill(len(fillers))
    scores(own, True)
    for k in (1, 2):
        x_copy(0, k, 0, k).wait_recv()
    go(x_half(1, 3, 0, 1))
    go(x_half(2, 3, 1, 2))
    sum_end(0)
    cos_p, sin_p = turned_tables(base_ref, start_ref, grp)
    kb[0] = rotate(mine[0], cos_p, sin_p).astype(BF)
    for k in range(1, NG):
        go(c_copy(0, k))
    sum_second(1)
    scores(0, False)

    def score_step(k, carry):
        c_copy(0, k).wait_recv()
        scores(k, False)
        return carry

    for k in range(1, 3):
        score_step(k, 0)
    sum_end(1)
    vb[0] = mine[1].astype(BF)
    for k in range(1, NG):
        go(c_copy(1, k))
    for k in range(3, NG):
        score_step(k, 0)
    m = functools.reduce(jnp.maximum, [top[p] for p in range(NG + 1)])
    weights = [jnp.exp2(top[p] - m) for p in range(NG + 1)]
    total = functools.reduce(jnp.add, [weights[p] * low[p] for p in range(NG + 1)])
    inverse = 1.0 / total
    for p in range(NG + 1):
        top[p] = weights[p] * inverse

    def e_copy(u, k):
        return remote(
            grad_send.at[u, k], grad_recv.at[u, k], e_ss.at[u, k], e_rs.at[u, k], on_grp(source(k))
        )

    def weigh(p):
        vt[p] = vb[p].astype(F32).T.astype(BF)
        dv = jnp.zeros((T, HD), F32)
        for c in range(GQ):
            ct = slice(c * T, (c + 1) * T)
            ab = (e[p, :, ct] * top[p, :, ct]).astype(BF)
            ds_all[p, :, ct] = ab
            dv = dv + dot(ab, g_rows[c])
        return dv

    def weigh_step(k, carry):
        c_copy(1, k).wait_recv()
        grad_send[1, k] = weigh(k).astype(BF)
        e_copy(1, k).start()
        return carry

    dkv_ref[:, HD:] = weigh(own).astype(BF)
    for k in range(1, NG):
        weigh_step(k, 0)
    mine[1] = weigh(0)
    for c in range(GQ):
        ct = slice(c * T, (c + 1) * T)
        out = jnp.zeros((HD, T), F32)
        for p in range(NG + 1):
            out = out + dot(vt[p], ds_all[p, :, ct])
        delta[:, ct] = jnp.sum(
            out.astype(BF).astype(F32) * g_cols[:, ct].astype(F32), axis=0, keepdims=True
        )

    def backward(p):
        v = vb[p]
        for c in range(GQ):
            ct = slice(c * T, (c + 1) * T)
            a = e[p, :, ct] * top[p, :, ct]
            da = dot(v, g_cols[:, ct])
            ds_all[p, :, ct] = (a * (da - delta[:, ct])).astype(BF)
        return dot(ds_all[p], q_rows[...].reshape(GQ * T, HD)) * SCALE

    def grad_step(i, carry):
        k = NG - 1 - i
        grad_send[0, k] = backward(k).astype(BF)
        e_copy(0, k).start()
        return carry

    def gather_sum(u):
        def step(i, carry):
            k = 1 + i if u == 1 else NG - 1 - i
            e_copy(u, k).wait_recv()
            mine[u] = mine[u] + grad_recv[u, k].astype(F32)
            return carry

        lax.fori_loop(0, NG - 1, step, 0)

    def f_copy(u, d, i):
        at = pl.ds(d * H, H) if i == 3 else pl.ds(0, T)
        step = (1, 2, 1, 2)[i]
        src = (0, 0, 2, 2)[i]
        dst = (1, 2, 3, 4)[i]
        if d == 0:
            src, dst = (nt - src) % nt, nt - dst
        return remote(
            heads.at[u, src, at], heads.at[u, dst, at], f_ss.at[u, d * 4 + i], f_rs.at[u, d * 4 + i],
            on_tp(step if d == 0 else -step),
        )

    def f_first(u):
        for i in (1, 0):
            for d in range(2):
                go(f_copy(u, d, i))
        pass_on(u, 0)

    def f_second(u):
        for d in range(2):
            f_copy(u, d, 1).wait_recv()
            for i in (3, 2):
                go(f_copy(u, d, i))
        for d in range(2):
            pass_on(u, nt - 2 if d == 0 else 2)
        for d in range(2):
            f_copy(u, d, 0).wait_recv()
            pass_on(u, nt - 1 if d == 0 else 1)

    def f_third(u):
        for d in range(2):
            f_copy(u, d, 2).wait_recv()
            pass_on(u, nt - 3 if d == 0 else 3)
        for d in range(2):
            f_copy(u, d, 3).wait_recv()
        pass_on(u, 4)

    def a_copy(u, slot):
        return remote(
            heads.at[u, slot], cols.at[u, grp], a_ss.at[u, slot], a_rs.at[u, grp], on_grp((tp + slot) % nt)
        )

    def pass_on(u, slot):
        @pl.when((tp + slot) % nt != grp)
        def _():
            a_copy(u, slot).start()

    def hidden(u, slot, first=False):
        h = (tp + slot) % nt
        at = pl.ds(pl.multiple_of(h * W2 + u * HD, HD), HD)
        term = lax.dot_general(
            heads[u, slot], w_ref[:, at], (((1,), (1,)), ((), ())), preferred_element_type=F32
        )
        if first:
            dh_acc[...] = term
        else:
            dh_acc[...] += term

    def query_out(c):
        ct = slice(c * T, (c + 1) * T)
        dq = jnp.zeros((HD, T), F32)
        for p in range(NG + 1):
            dq = dq + dot(kt[p], ds_all[p, :, ct])
        dq_ref[:, c * HD : (c + 1) * HD] = rotate(dq.T * SCALE, cos_r[...], -sin_r[...]).astype(BF)

    for i in range(3):
        grad_step(i, 0)
    gather_sum(1)
    heads[1, 0] = mine[1].astype(BF)
    f_first(1)
    for i in range(3, NG - 1):
        grad_step(i, 0)
    mine[0] = backward(0)
    f_second(1)
    x_copy(0, 4, 0, 4).wait_recv()
    go(x_copy(4, 5, 0, 1))
    go(x_copy(4, 6, 0, 2))
    for i in range(2):
        x_half(1, 3, i, 1).wait_recv()
    go(x_copy(3, 7, 0, 4))
    gather_sum(0)
    cos_p, sin_p = turned_tables(base_ref, start_ref, grp)
    heads[0, 0] = rotate(mine[0], cos_p, -sin_p).astype(BF)
    f_first(0)
    f_third(1)
    dk = backward(own)
    dkv_ref[:, :HD] = rotate(dk, cos_r[...], -sin_r[...]).astype(BF)
    stores = [
        pltpu.make_async_copy(src, dst, out_sems.at[i])
        for i, (src, dst) in enumerate(
            [
                (dkv_ref, dkv_out),
                (dq_ref, dq_out),
                (dh_ref, dh_out),
                (dw_ref.at[:, pl.ds(HD, HD)], dw_out.at[:, pl.ds(HD, HD)]),
                (dw_ref.at[:, pl.ds(0, HD)], dw_out.at[:, pl.ds(0, HD)]),
            ]
        )
    ]
    stores[0].start()
    f_second(0)
    for c in range(4):
        query_out(c)
    f_third(0)
    for c in range(4, GQ):
        query_out(c)
    stores[1].start()
    hidden(1, 0, True)
    for slot in range(1, nt):
        hidden(1, slot)
    for slot in range(nt):
        hidden(0, slot)

    def weights_out(u):
        def arrived(k, carry):
            other = source(k)
            remote(
                heads.at[u, 0], cols.at[u, other], a_ss.at[u, 0], a_rs.at[u, other], on_grp(peer(1))
            ).wait_recv()
            return carry

        lax.fori_loop(1, NG, arrived, 0)
        cols[u, grp] = heads[u, (grp - tp + nt) % nt]
        for i in range(2):
            at = slice(i * D // 2, (i + 1) * D // 2)
            total = dot(x_t[0, at], cols[u, grp])
            for k in range(1, NG):
                total = total + dot(x_t[k, at], cols[u, source(k)])
            dw_ref[at, u * HD : (u + 1) * HD] = total

    dh_ref[...] = dh_acc[...].astype(BF)
    stores[2].start()
    for k in (5, 6, 7):
        x_copy(4, k, 0, 1).wait_recv()
    weights_out(1)
    stores[3].start()
    weights_out(0)
    stores[4].start()

    for copy in started:
        copy.wait_send()

    def end_step(k, carry):
        e_copy(0, k).wait_send()
        e_copy(1, k).wait_send()
        return carry

    lax.fori_loop(1, NG, end_step, 0)
    for slot in range(nt):

        @pl.when((tp + slot) % nt != grp)
        def _():
            a_copy(0, slot).wait_send()
            a_copy(1, slot).wait_send()

    for store in stores:
        store.wait()


def hand_over(*refs):
    n = len(refs) // 2
    for i in range(n):
        refs[n + i][...] = refs[i][...]


def local(nx, nt, prompt_hidden, w_kv, resp_q, resp_kv, d_out, lengths):
    T, D = prompt_hidden.shape
    NG = 2 * nx
    W2 = 2 * HD
    base, start = tables(T, NG + 1)
    start = start[:, None]
    vm = pl.BlockSpec(memory_space=pltpu.VMEM)
    hbm = pl.BlockSpec(memory_space=pl.ANY)
    dma = pltpu.SemaphoreType.DMA
    results = pl.pallas_call(
        functools.partial(kernel, nx, nt),
        out_shape=(
            jax.ShapeDtypeStruct((T, GQ * HD), BF),
            jax.ShapeDtypeStruct((T, W2), BF),
            jax.ShapeDtypeStruct((T, D), BF),
            jax.ShapeDtypeStruct((D, W2), F32),
        ),
        in_specs=[hbm] * 5 + [pl.BlockSpec(memory_space=pltpu.SMEM)] + [hbm, vm],
        out_specs=(hbm,) * 4,
        scratch_shapes=[
            pltpu.VMEM((T, D), BF),
            pltpu.VMEM((D, nt * W2), BF),
            pltpu.VMEM((T, GQ * HD), BF),
            pltpu.VMEM((T, GQ * HD), BF),
            pltpu.VMEM((T, W2), BF),
            pltpu.VMEM((T, W2), F32),
            pltpu.VMEM((T, GQ * HD), BF),
            pltpu.VMEM((T, W2), BF),
            pltpu.VMEM((T, D), BF),
            pltpu.VMEM((D, W2), F32),
            pltpu.VMEM((GQ, T, HD), BF),
            pltpu.VMEM((HD, GQ * T), BF),
            pltpu.VMEM((GQ, T, HD), BF),
            pltpu.VMEM((HD, GQ * T), BF),
            pltpu.VMEM((NG + 1, T, HD), BF),
            pltpu.VMEM((NG + 1, T, HD), BF),
            pltpu.VMEM((NG + 1, HD, T), BF),
            pltpu.VMEM((NG + 1, HD, T), BF),
            pltpu.VMEM((NG + 1, T, GQ * T), F32),
            pltpu.VMEM((NG + 1, 1, GQ * T), F32),
            pltpu.VMEM((NG + 1, 1, GQ * T), F32),
            pltpu.VMEM((1, GQ * T), F32),
            pltpu.VMEM((NG + 1, T, GQ * T), BF),
            pltpu.VMEM((T, HD), F32),
            pltpu.VMEM((T, HD), F32),
            pltpu.VMEM((2, 2, 4, T, HD), BF),
            pltpu.VMEM((2, 2, 4, T, HD), BF),
            pltpu.VMEM((2, 2, T, HD), F32),
            pltpu.VMEM((2, T, HD), F32),
            pltpu.VMEM((NG, D, T), BF),
            pltpu.VMEM((2, NG, T, HD), BF),
            pltpu.VMEM((2, NG, T, HD), BF),
            pltpu.VMEM((2, nt, T, HD), BF),
            pltpu.VMEM((2, NG, T, HD), BF),
            pltpu.VMEM((T, D), F32),
            dma((2, 2, 4)),
            dma((2, 2, 4)),
            dma((NG, 2)),
            dma((NG, 2)),
            dma((2, NG)),
            dma((2, NG)),
            dma((2, NG)),
            dma((2, NG)),
            dma((2, nt)),
            dma((2, nt)),
            dma((2, nt)),
            dma((2, NG)),
            dma((6,)),
            dma((5,)),
        ],
        compiler_params=pltpu.CompilerParams(
            collective_id=0, has_side_effects=True, vmem_limit_bytes=60 * 2**20
        ),
        name="prefix_attention_backward",
    )(
        prompt_hidden,
        w_kv,
        resp_q.reshape(T, GQ * HD),
        d_out.reshape(T, GQ * HD),
        resp_kv.reshape(T, W2),
        lengths,
        jnp.asarray(base),
        jnp.asarray(start),
    )
    dq, dkv, dh, dw = pl.pallas_call(
        hand_over,
        out_shape=tuple(jax.ShapeDtypeStruct(r.shape, r.dtype) for r in results),
        in_specs=[vm] * 4,
        out_specs=(vm,) * 4,
        name="hand_over",
    )(*results)
    return dq[None], dkv[None], dh, dw


def solution(mesh):
    nx = mesh.shape["grp"] // 2
    nt = mesh.shape["tp"]
    return jax.shard_map(
        functools.partial(local, nx, nt),
        mesh=mesh,
        in_specs=(
            P(("dp", "grp"), "tp"),
            P("tp", None),
            P(("dp", "grp"), None, "tp"),
            P(("dp", "grp"), None, "tp"),
            P(("dp", "grp"), None, "tp"),
            P(("dp", "grp")),
        ),
        out_specs=(
            P(("dp", "grp"), None, "tp"),
            P(("dp", "grp"), None, "tp"),
            P(("dp", "grp"), "tp"),
            P(("dp", "tp"), "grp"),
        ),
        check_vma=False,
    )
```

```python
import functools

import jax
import jax.numpy as jnp
import numpy as np
from jax import lax
from jax.experimental import pallas as pl
from jax.experimental.pallas import tpu as pltpu
from jax.sharding import PartitionSpec as P

HD = 128
GQ = 8
THETA = 1000000.0
SCALE = HD**-0.5
SCALE2 = SCALE * float(np.log2(np.e))
MESH = pl.DeviceIdType.MESH
BF = jnp.bfloat16
F32 = jnp.float32


def tables(rows, groups):
    ladder = np.arange(HD // 2)
    frequency = (THETA ** (-2.0 * ladder / HD)).astype(np.float32).astype(np.float64)

    def both(positions):
        turned = positions[:, None] * frequency[None, :]
        cos, sin = np.cos(turned), np.sin(turned)
        return np.concatenate([cos, cos, -sin, sin], 1).astype(np.float32)

    return both(np.arange(rows)), both(np.arange(groups) * rows)


def dot(a, b):
    return lax.dot_general(a, b, (((1,), (0,)), ((), ())), preferred_element_type=F32)


def rotate(v, cos, sin):
    return v * cos + pltpu.roll(v, HD // 2, 1) * sin


def turned_tables(base_ref, start_ref, block):
    cos, sin = base_ref[:, :HD], base_ref[:, HD:]
    turn = start_ref[block]
    cos0, sin0 = turn[:, :HD], turn[:, HD:]
    return cos * cos0 - sin * sin0, sin * cos0 + cos * sin0


def kernel(
    nx, nt, x_in, w_in, q_in, do_in, kv_in, len_ref, base_in, start_ref,
    dq_out, dkv_out, dh_out, dw_out,
    x_ref, w_ref, q_ref, do_ref, kv_ref, base_ref, dq_ref, dkv_ref, dh_ref, dw_ref,
    q_rows, q_cols, g_rows, g_cols, kb, vb, kt, vt, e, top, low, delta, ds_all, cos_r, sin_r,
    b_send, b_recv, raw, mine, x_t, grad_send, grad_recv, heads, cols, dh_acc,
    b_ss, b_rs, x_ss, x_rs, c_ss, c_rs, e_ss, e_rs, f_ss, f_rs, a_ss, a_rs, in_sems, out_sems,
):
    T = x_ref.shape[0]
    D = x_ref.shape[1]
    H = T // 2
    W2 = 2 * HD
    NG = 2 * nx
    own = NG
    kv = (kb, vb)
    grp, tp, dp = lax.axis_index("grp"), lax.axis_index("tp"), lax.axis_index("dp")
    x, y = grp // 2, grp % 2

    def offset(k):
        j = k % 4
        return j + j // 2 - 2 * (j // 3), k // 4

    def peer(k):
        dx, dy = offset(k)
        return ((x + dx) % nx) * 2 + (y + dy) % 2

    def source(k):
        dx, dy = offset(k)
        return ((x - dx + nx) % nx) * 2 + (y + dy) % 2

    def on_grp(other):
        return (other, tp, dp)

    def on_tp(step):
        return (grp, (tp + step + nt) % nt, dp)

    def remote(src, dst, ss, rs, device):
        return pltpu.make_async_remote_copy(
            src_ref=src, dst_ref=dst, send_sem=ss, recv_sem=rs, device_id=device, device_id_type=MESH
        )

    started = []

    def go(copy):
        copy.start()
        started.append(copy)

    barrier = pltpu.get_barrier_semaphore()
    for k in range(1, NG):
        pl.semaphore_signal(barrier, inc=1, device_id=on_grp(peer(k)), device_id_type=MESH)
    for step in range(1, nt):
        pl.semaphore_signal(barrier, inc=1, device_id=on_tp(step), device_id_type=MESH)

    loads = [
        pltpu.make_async_copy(src, dst, in_sems.at[i])
        for i, (src, dst) in enumerate(
            [(x_in, x_ref), (w_in, w_ref), (base_in, base_ref), (q_in, q_ref), (do_in, do_ref), (kv_in, kv_ref)]
        )
    ]
    for load in loads:
        load.start()

    def part(h, u):
        at = pl.ds(pl.multiple_of(h * W2 + u * HD, HD), HD)
        return dot(x_ref[...], w_ref[:, at])

    def b_copy(u, d, i):
        step = (2, 1, 1, 2)[i]
        at = pl.ds(d * H, H) if i == 0 else pl.ds(0, T)
        return remote(
            b_send.at[u, d, i, at], b_recv.at[u, d, i, at], b_ss.at[u, d, i], b_rs.at[u, d, i],
            on_tp(step if d == 0 else -step),
        )

    def x_copy(src, dst, i, to):
        return remote(x_t.at[src], x_t.at[dst], x_ss.at[dst, i], x_rs.at[dst, i], on_grp(peer(to)))

    def x_half(src, dst, i, to):
        at = pl.ds(i * (D // 2), D // 2)
        return remote(
            x_t.at[src, at], x_t.at[dst, at], x_ss.at[dst, i], x_rs.at[dst, i], on_grp(peer(to))
        )

    def sum_first(u):
        far = part((tp + 4) % nt, u).astype(BF)
        for d in range(2):
            b_send[u, d, 0, d * H : (d + 1) * H] = far[d * H : (d + 1) * H]
            b_send[u, d, 1] = part((tp + (3 if d == 0 else nt - 3)) % nt, u).astype(BF)

    def sum_send(u):
        for i in range(2):
            for d in range(2):
                go(b_copy(u, d, i))

    def sum_near(u):
        for d in range(2):
            b_send[u, d, 2] = part((tp + (1 if d == 0 else nt - 1)) % nt, u).astype(BF)
            go(b_copy(u, d, 2))
        for d in range(2):
            raw[u, d] = part((tp + (2 if d == 0 else nt - 2)) % nt, u)
        mine[u] = part(tp, u)

    def sum_second(u):
        for d in range(2):
            at = slice(d * H, (d + 1) * H)
            b_copy(u, d, 0).wait_recv()
            raw[u, d, at] = raw[u, d, at] + b_recv[u, d, 0, at].astype(F32)
            b_copy(u, d, 1).wait_recv()
            b_send[u, d, 3] = (raw[u, d] + b_recv[u, d, 1].astype(F32)).astype(BF)
            go(b_copy(u, d, 3))

    def sum_end(u):
        total = mine[u]
        for i in (2, 3):
            for d in range(2):
                b_copy(u, d, i).wait_recv()
                total = total + b_recv[u, d, i].astype(F32)
        mine[u] = total

    def c_copy(u, k):
        return remote(kv[u].at[0], kv[u].at[k], c_ss.at[u, k], c_rs.at[u, k], on_grp(peer(k)))

    loads[0].wait()
    x_t[0] = x_ref[...].astype(F32).T.astype(BF)
    loads[1].wait()
    sum_first(0)
    pl.semaphore_wait(barrier, NG - 1 + nt - 1)
    sum_send(0)
    sum_near(0)
    for k in (1, 2, 4):
        go(x_copy(0, k, 0, k))

    def prep_tables():
        c, s = turned_tables(base_ref, start_ref, NG)
        cos_r[...] = c
        sin_r[...] = s

    def prep(c):
        def run():
            at = slice(c * HD, (c + 1) * HD)
            ct = slice(c * T, (c + 1) * T)
            live = lax.broadcasted_iota(jnp.int32, (T, HD), 0) < len_ref[0]
            qf = rotate(q_ref[:, at].astype(F32), cos_r[...], sin_r[...])
            q_rows[c] = qf.astype(BF)
            q_cols[:, ct] = qf.T.astype(BF)
            gf = jnp.where(live, do_ref[:, at].astype(F32), 0.0)
            g_rows[c] = gf.astype(BF)
            g_cols[:, ct] = gf.T.astype(BF)

        return run

    def prep_own():
        kb[own] = rotate(kv_ref[:, :HD].astype(F32), cos_r[...], sin_r[...]).astype(BF)
        vb[own] = kv_ref[:, HD:]

    def scores(p, is_own):
        kt[p] = kb[p].astype(F32).T.astype(BF)
        k = kb[p]
        if is_own:
            visible = lax.broadcasted_iota(jnp.int32, (T, T), 0) <= lax.broadcasted_iota(
                jnp.int32, (T, T), 1
            )
        for c in range(GQ):
            ct = slice(c * T, (c + 1) * T)
            s = dot(k, q_cols[:, ct])
            if is_own:
                s = jnp.where(visible, s, -jnp.inf)
            m = jnp.max(s, axis=0, keepdims=True) * SCALE2
            raised = jnp.exp2(s * SCALE2 - m)
            e[p, :, ct] = raised
            top[p, :, ct] = m
            low[p, :, ct] = jnp.sum(raised, axis=0, keepdims=True)

    fillers = [prep_tables] + [prep(c) for c in range(GQ)] + [prep_own]

    def fill(count):
        for _ in range(count):
            if fillers:
                fillers.pop(0)()

    for load in loads[2:]:
        load.wait()
    fill(4)
    sum_second(0)
    sum_first(1)
    sum_send(1)
    sum_near(1)
    fill(len(fillers))
    scores(own, True)
    sum_end(0)
    cos_p, sin_p = turned_tables(base_ref, start_ref, grp)
    kb[0] = rotate(mine[0], cos_p, sin_p).astype(BF)
    for k in range(1, NG):
        go(c_copy(0, k))
    sum_second(1)
    scores(0, False)

    def score_step(k, carry):
        c_copy(0, k).wait_recv()
        scores(k, False)
        return carry

    for k in range(1, 3):
        score_step(k, 0)
    sum_end(1)
    vb[0] = mine[1].astype(BF)
    for k in range(1, NG):
        go(c_copy(1, k))
    for k in (1, 2):
        x_copy(0, k, 0, k).wait_recv()
    go(x_half(1, 3, 0, 1))
    go(x_half(2, 3, 1, 2))
    for k in range(3, NG):
        score_step(k, 0)
    m = functools.reduce(jnp.maximum, [top[p] for p in range(NG + 1)])
    weights = [jnp.exp2(top[p] - m) for p in range(NG + 1)]
    total = functools.reduce(jnp.add, [weights[p] * low[p] for p in range(NG + 1)])
    inverse = 1.0 / total
    for p in range(NG + 1):
        top[p] = weights[p] * inverse

    def e_copy(u, k):
        return remote(
            grad_send.at[u, k], grad_recv.at[u, k], e_ss.at[u, k], e_rs.at[u, k], on_grp(source(k))
        )

    def weigh(p):
        vt[p] = vb[p].astype(F32).T.astype(BF)
        dv = jnp.zeros((T, HD), F32)
        for c in range(GQ):
            ct = slice(c * T, (c + 1) * T)
            ab = (e[p, :, ct] * top[p, :, ct]).astype(BF)
            ds_all[p, :, ct] = ab
            dv = dv + dot(ab, g_rows[c])
        return dv

    def weigh_step(k, carry):
        c_copy(1, k).wait_recv()
        grad_send[1, k] = weigh(k).astype(BF)
        e_copy(1, k).start()
        return carry

    dkv_ref[:, HD:] = weigh(own).astype(BF)
    mine[1] = weigh(0)
    for k in range(1, NG):
        weigh_step(k, 0)
    for c in range(GQ):
        ct = slice(c * T, (c + 1) * T)
        out = jnp.zeros((HD, T), F32)
        for p in range(NG + 1):
            out = out + dot(vt[p], ds_all[p, :, ct])
        delta[:, ct] = jnp.sum(
            out.astype(BF).astype(F32) * g_cols[:, ct].astype(F32), axis=0, keepdims=True
        )

    def backward(p):
        v = vb[p]
        for c in range(GQ):
            ct = slice(c * T, (c + 1) * T)
            a = e[p, :, ct] * top[p, :, ct]
            da = dot(v, g_cols[:, ct])
            ds_all[p, :, ct] = (a * (da - delta[:, ct])).astype(BF)
        return dot(ds_all[p], q_rows[...].reshape(GQ * T, HD)) * SCALE

    def grad_step(i, carry):
        k = NG - 1 - i
        grad_send[0, k] = backward(k).astype(BF)
        e_copy(0, k).start()
        return carry

    def gather_sum(u):
        def step(i, carry):
            k = 1 + i if u == 1 else NG - 1 - i
            e_copy(u, k).wait_recv()
            mine[u] = mine[u] + grad_recv[u, k].astype(F32)
            return carry

        lax.fori_loop(0, NG - 1, step, 0)

    def f_copy(u, d, i):
        at = pl.ds(d * H, H) if i == 3 else pl.ds(0, T)
        step = (1, 2, 1, 2)[i]
        src = (0, 0, 2, 2)[i]
        dst = (1, 2, 3, 4)[i]
        if d == 0:
            src, dst = (nt - src) % nt, nt - dst
        return remote(
            heads.at[u, src, at], heads.at[u, dst, at], f_ss.at[u, d * 4 + i], f_rs.at[u, d * 4 + i],
            on_tp(step if d == 0 else -step),
        )

    def f_first(u):
        for i in (1, 0):
            for d in range(2):
                go(f_copy(u, d, i))
        pass_on(u, 0)

    def f_second(u):
        for d in range(2):
            f_copy(u, d, 1).wait_recv()
            for i in (3, 2):
                go(f_copy(u, d, i))
        for d in range(2):
            pass_on(u, nt - 2 if d == 0 else 2)
        for d in range(2):
            f_copy(u, d, 0).wait_recv()
            pass_on(u, nt - 1 if d == 0 else 1)

    def f_third(u):
        for d in range(2):
            f_copy(u, d, 2).wait_recv()
            pass_on(u, nt - 3 if d == 0 else 3)
        for d in range(2):
            f_copy(u, d, 3).wait_recv()
        pass_on(u, 4)

    def a_copy(u, slot):
        return remote(
            heads.at[u, slot], cols.at[u, grp], a_ss.at[u, slot], a_rs.at[u, grp], on_grp((tp + slot) % nt)
        )

    def pass_on(u, slot):
        @pl.when((tp + slot) % nt != grp)
        def _():
            a_copy(u, slot).start()

    def hidden(u, slot, first=False):
        h = (tp + slot) % nt
        at = pl.ds(pl.multiple_of(h * W2 + u * HD, HD), HD)
        term = lax.dot_general(
            heads[u, slot], w_ref[:, at], (((1,), (1,)), ((), ())), preferred_element_type=F32
        )
        if first:
            dh_acc[...] = term
        else:
            dh_acc[...] += term

    def query_out(c):
        ct = slice(c * T, (c + 1) * T)
        dq = jnp.zeros((HD, T), F32)
        for p in range(NG + 1):
            dq = dq + dot(kt[p], ds_all[p, :, ct])
        dq_ref[:, c * HD : (c + 1) * HD] = rotate(dq.T * SCALE, cos_r[...], -sin_r[...]).astype(BF)

    for i in range(6):
        grad_step(i, 0)
    gather_sum(1)
    heads[1, 0] = mine[1].astype(BF)
    f_first(1)
    for i in range(6, NG - 1):
        grad_step(i, 0)
    mine[0] = backward(0)
    f_second(1)
    x_copy(0, 4, 0, 4).wait_recv()
    go(x_copy(4, 5, 0, 1))
    go(x_copy(4, 6, 0, 2))
    for i in range(2):
        x_half(1, 3, i, 1).wait_recv()
    go(x_copy(3, 7, 0, 4))
    gather_sum(0)
    cos_p, sin_p = turned_tables(base_ref, start_ref, grp)
    heads[0, 0] = rotate(mine[0], cos_p, -sin_p).astype(BF)
    f_first(0)
    f_third(1)
    dk = backward(own)
    dkv_ref[:, :HD] = rotate(dk, cos_r[...], -sin_r[...]).astype(BF)
    stores = [
        pltpu.make_async_copy(src, dst, out_sems.at[i])
        for i, (src, dst) in enumerate(
            [
                (dkv_ref, dkv_out),
                (dq_ref, dq_out),
                (dh_ref, dh_out),
                (dw_ref.at[:, pl.ds(HD, HD)], dw_out.at[:, pl.ds(HD, HD)]),
                (dw_ref.at[:, pl.ds(0, HD)], dw_out.at[:, pl.ds(0, HD)]),
            ]
        )
    ]
    stores[0].start()
    f_second(0)
    for c in range(4):
        query_out(c)
    f_third(0)
    for c in range(4, GQ):
        query_out(c)
    stores[1].start()
    hidden(1, 0, True)
    for slot in range(1, nt):
        hidden(1, slot)
    for slot in range(nt):
        hidden(0, slot)

    def weights_out(u):
        def arrived(k, carry):
            other = source(k)
            remote(
                heads.at[u, 0], cols.at[u, other], a_ss.at[u, 0], a_rs.at[u, other], on_grp(peer(1))
            ).wait_recv()
            return carry

        lax.fori_loop(1, NG, arrived, 0)
        cols[u, grp] = heads[u, (grp - tp + nt) % nt]
        for i in range(2):
            at = slice(i * D // 2, (i + 1) * D // 2)
            total = dot(x_t[0, at], cols[u, grp])
            for k in range(1, NG):
                total = total + dot(x_t[k, at], cols[u, source(k)])
            dw_ref[at, u * HD : (u + 1) * HD] = total

    dh_ref[...] = dh_acc[...].astype(BF)
    stores[2].start()
    for k in (5, 6, 7):
        x_copy(4, k, 0, 1).wait_recv()
    weights_out(1)
    stores[3].start()
    weights_out(0)
    stores[4].start()

    for copy in started:
        copy.wait_send()

    def end_step(k, carry):
        e_copy(0, k).wait_send()
        e_copy(1, k).wait_send()
        return carry

    lax.fori_loop(1, NG, end_step, 0)
    for slot in range(nt):

        @pl.when((tp + slot) % nt != grp)
        def _():
            a_copy(0, slot).wait_send()
            a_copy(1, slot).wait_send()

    for store in stores:
        store.wait()


def hand_over(*refs):
    n = len(refs) // 2
    for i in range(n):
        refs[n + i][...] = refs[i][...]


def local(nx, nt, prompt_hidden, w_kv, resp_q, resp_kv, d_out, lengths):
    T, D = prompt_hidden.shape
    NG = 2 * nx
    W2 = 2 * HD
    base, start = tables(T, NG + 1)
    start = start[:, None]
    vm = pl.BlockSpec(memory_space=pltpu.VMEM)
    hbm = pl.BlockSpec(memory_space=pl.ANY)
    dma = pltpu.SemaphoreType.DMA
    results = pl.pallas_call(
        functools.partial(kernel, nx, nt),
        out_shape=(
            jax.ShapeDtypeStruct((T, GQ * HD), BF),
            jax.ShapeDtypeStruct((T, W2), BF),
            jax.ShapeDtypeStruct((T, D), BF),
            jax.ShapeDtypeStruct((D, W2), F32),
        ),
        in_specs=[hbm] * 5 + [pl.BlockSpec(memory_space=pltpu.SMEM)] + [hbm, vm],
        out_specs=(hbm,) * 4,
        scratch_shapes=[
            pltpu.VMEM((T, D), BF),
            pltpu.VMEM((D, nt * W2), BF),
            pltpu.VMEM((T, GQ * HD), BF),
            pltpu.VMEM((T, GQ * HD), BF),
            pltpu.VMEM((T, W2), BF),
            pltpu.VMEM((T, W2), F32),
            pltpu.VMEM((T, GQ * HD), BF),
            pltpu.VMEM((T, W2), BF),
            pltpu.VMEM((T, D), BF),
            pltpu.VMEM((D, W2), F32),
            pltpu.VMEM((GQ, T, HD), BF),
            pltpu.VMEM((HD, GQ * T), BF),
            pltpu.VMEM((GQ, T, HD), BF),
            pltpu.VMEM((HD, GQ * T), BF),
            pltpu.VMEM((NG + 1, T, HD), BF),
            pltpu.VMEM((NG + 1, T, HD), BF),
            pltpu.VMEM((NG + 1, HD, T), BF),
            pltpu.VMEM((NG + 1, HD, T), BF),
            pltpu.VMEM((NG + 1, T, GQ * T), F32),
            pltpu.VMEM((NG + 1, 1, GQ * T), F32),
            pltpu.VMEM((NG + 1, 1, GQ * T), F32),
            pltpu.VMEM((1, GQ * T), F32),
            pltpu.VMEM((NG + 1, T, GQ * T), BF),
            pltpu.VMEM((T, HD), F32),
            pltpu.VMEM((T, HD), F32),
            pltpu.VMEM((2, 2, 4, T, HD), BF),
            pltpu.VMEM((2, 2, 4, T, HD), BF),
            pltpu.VMEM((2, 2, T, HD), F32),
            pltpu.VMEM((2, T, HD), F32),
            pltpu.VMEM((NG, D, T), BF),
            pltpu.VMEM((2, NG, T, HD), BF),
            pltpu.VMEM((2, NG, T, HD), BF),
            pltpu.VMEM((2, nt, T, HD), BF),
            pltpu.VMEM((2, NG, T, HD), BF),
            pltpu.VMEM((T, D), F32),
            dma((2, 2, 4)),
            dma((2, 2, 4)),
            dma((NG, 2)),
            dma((NG, 2)),
            dma((2, NG)),
            dma((2, NG)),
            dma((2, NG)),
            dma((2, NG)),
            dma((2, nt)),
            dma((2, nt)),
            dma((2, nt)),
            dma((2, NG)),
            dma((6,)),
            dma((5,)),
        ],
        compiler_params=pltpu.CompilerParams(
            collective_id=0, has_side_effects=True, vmem_limit_bytes=60 * 2**20
        ),
        name="prefix_attention_backward",
    )(
        prompt_hidden,
        w_kv,
        resp_q.reshape(T, GQ * HD),
        d_out.reshape(T, GQ * HD),
        resp_kv.reshape(T, W2),
        lengths,
        jnp.asarray(base),
        jnp.asarray(start),
    )
    dq, dkv, dh, dw = pl.pallas_call(
        hand_over,
        out_shape=tuple(jax.ShapeDtypeStruct(r.shape, r.dtype) for r in results),
        in_specs=[vm] * 4,
        out_specs=(vm,) * 4,
        name="hand_over",
    )(*results)
    return dq[None], dkv[None], dh, dw


def solution(mesh):
    nx = mesh.shape["grp"] // 2
    nt = mesh.shape["tp"]
    return jax.shard_map(
        functools.partial(local, nx, nt),
        mesh=mesh,
        in_specs=(
            P(("dp", "grp"), "tp"),
            P("tp", None),
            P(("dp", "grp"), None, "tp"),
            P(("dp", "grp"), None, "tp"),
            P(("dp", "grp"), None, "tp"),
            P(("dp", "grp")),
        ),
        out_specs=(
            P(("dp", "grp"), None, "tp"),
            P(("dp", "grp"), None, "tp"),
            P(("dp", "grp"), "tp"),
            P(("dp", "tp"), "grp"),
        ),
        check_vma=False,
    )
```
